32 devices in a mesh: groups: 2 (over y), ctx: 4 (over z), head: 4 (over x, core).
Axes of the slice: x: 2, y: 2, z: 4, core: 2. Of those that a mesh axis runs over, the one named last changes fastest.
Arguments:
- hidden: bfloat16 [1024, 7168], P(('groups', 'ctx'), 'head'), parts along dimension 0, may hold values from -210 to 210
- q_latent: bfloat16 [1024, 1536], P(('groups', 'ctx')), parts along dimension 0, may hold values from -210 to 210
- w_down: bfloat16 [7168, 576], P('head'), may hold values from -0.0625 to 0.0625
- latent_gain: float32 [512], replicated, may hold values from 0.1 to 1.9
- w_qup: bfloat16 [1536, 12288], P(None, 'head'), may hold values from -0.15625 to 0.15625
- w_kvup: bfloat16 [512, 16384], P(None, 'head'), may hold values from -0.25 to 0.25
- w_out: bfloat16 [8192, 7168], P('head', 'ctx'), may hold values from -0.0625 to 0.0625
Outputs:
- mixed: bfloat16 [1024, 7168], P(('groups', 'head'), 'ctx'), parts along dimension 0
The draws below stay inside these ranges and needn't reach their ends.
There are 2 independent parts, one for each index of `groups`. The reference program is written for one: setup_inputs(seed, part) draws one part's arguments, and reference() takes and returns one part's arrays. A program takes and returns all parts, laid end to end along the dimension named above; an argument that names none is the same for every part. Nothing has to cross between parts.
All inputs are finite; a program needn't handle non-finite values.
Results may differ from the reference program's by a relative error of at most 0.012.
The reference program's roundings to bfloat16 on the way (of `latent`, `rope_key`, `query`, `keyval`, `weights` and `attended`) count: a program that leaves them out, or rounds other values in their place, can miss the bound.
Values may be sent and summed in bfloat16 or wider, within the bound.
A program may use at most 128 MiB of HBM per device.

```python
import math
import jax
import jax.numpy as jnp
from jax import lax

D = 7168
HEADS = 64
NOPE = 128
ROPE = 64
VDIM = 128
KVRANK = 512
QRANK = 1536
TOKENS = 512


def draw_hidden(key, part):
    key = jax.random.fold_in(key, 11)
    return jnp.clip(jax.random.normal(key, (TOKENS, D)), -6.0, 6.0).astype(jnp.bfloat16)


def draw_q_latent(key, part):
    key = jax.random.fold_in(key, 23)
    return jnp.clip(jax.random.normal(key, (TOKENS, QRANK)), -6.0, 6.0).astype(jnp.bfloat16)


def steps_of(own_key, shape, cuts, least, high):
    level = 1.0
    for dim, blocks in cuts:
        heights = jax.random.uniform(jax.random.fold_in(jax.random.fold_in(own_key, 6), dim), (blocks,), jnp.float32, least / len(cuts), high / len(cuts))
        level = level * jnp.repeat(jnp.exp(heights), shape[dim] // blocks).reshape((-1,) + (1,) * (len(shape) - 1 - dim))
    return level


def scatter_about(rng, shape, scale, reach, cuts=(), kind=jnp.bfloat16):
    array = scale * jax.random.normal(rng, shape, jnp.float32)
    if cuts:
        array = array * steps_of(rng, shape, cuts, -0.22, 0.18)
    return jnp.clip(array, -reach, reach).astype(kind)


def setup_inputs(seed: int = 0, part: int = 0) -> dict:
    seeds = jax.random.split(jax.random.key(seed), 8)
    part_splits = jax.random.split(jax.random.fold_in(seeds[7], part), 8)
    hidden = draw_hidden(jax.random.fold_in(jax.random.fold_in(seeds[7], part), 71), part)
    q_latent = draw_q_latent(jax.random.fold_in(jax.random.fold_in(seeds[7], part), 71), part)
    w_down = scatter_about(seeds[2], (D, KVRANK + ROPE), D ** -0.5, 0.0625, ((0, 4),))
    latent_gain = jnp.clip(1.0 + 0.18 * jax.random.normal(seeds[3], (KVRANK,), jnp.float32), 0.1, 1.9)
    w_qup = scatter_about(seeds[4], (QRANK, HEADS * (NOPE + ROPE)), QRANK ** -0.5, 0.15625, ((1, 4),))
    w_kvup = scatter_about(seeds[5], (KVRANK, HEADS * (NOPE + VDIM)), KVRANK ** -0.5, 0.25, ((1, 4),))
    w_out = scatter_about(seeds[6], (HEADS * VDIM, D), (HEADS * VDIM) ** -0.5, 0.0625, ((0, 4), (1, 4)))
    return dict(hidden=hidden, q_latent=q_latent, w_down=w_down, latent_gain=latent_gain, w_qup=w_qup, w_kvup=w_kvup, w_out=w_out)


def rotate(pairs, position):
    half = pairs.shape[-1] // 2
    freqs = jnp.exp(jnp.arange(half, dtype=jnp.float32) * (-2.0 * math.log(10000.0) / pairs.shape[-1]))
    angle = position[..., None] * freqs
    first_half = pairs[..., :half]
    second_half = pairs[..., half:]
    return jnp.concatenate([first_half * jnp.cos(angle) - second_half * jnp.sin(angle), first_half * jnp.sin(angle) + second_half * jnp.cos(angle)], -1)

def reference(hidden, q_latent, w_down, latent_gain, w_qup, w_kvup, w_out):
    count = hidden.shape[0]
    position = jnp.arange(count, dtype=jnp.int32).astype(jnp.float32)
    compressed = jnp.dot(hidden, w_down, preferred_element_type=jnp.float32)
    lat_part = compressed[:, :KVRANK]
    latent = (lat_part * lax.rsqrt(lax.optimization_barrier(jnp.mean(lat_part * lat_part, -1, keepdims=True)) + 1e-06) * latent_gain).astype(jnp.bfloat16)
    rope_key = rotate(compressed[:, KVRANK:], position).astype(jnp.bfloat16)
    query = jnp.dot(q_latent, w_qup, preferred_element_type=jnp.float32).reshape(count, HEADS, NOPE + ROPE)
    query = jnp.concatenate([query[..., :NOPE], rotate(query[..., NOPE:], position[:, None])], -1).astype(jnp.bfloat16)
    keyval = jnp.dot(latent, w_kvup, preferred_element_type=jnp.float32).astype(jnp.bfloat16).reshape(count, HEADS, NOPE + VDIM)
    allowed = position[:, None] >= position[None, :]
    scale = (NOPE + ROPE) ** (-0.5)
    rope_wide = rope_key.astype(jnp.float32)

    def one_head(operands):
        head_query, head_kv = operands
        values = head_kv[:, NOPE:]
        head_query = head_query.astype(jnp.float32)
        head_wide = head_kv.astype(jnp.float32)
        scores = jnp.dot(head_query[:, :NOPE], head_wide[:, :NOPE].T, precision=lax.Precision.HIGHEST)
        scores = scores + jnp.dot(head_query[:, NOPE:], rope_wide.T, precision=lax.Precision.HIGHEST)
        scores = jnp.where(allowed, scores * scale, -1e+30)
        row_max = lax.optimization_barrier(jnp.max(scores, -1, keepdims=True))
        probs = jnp.where(allowed, jnp.exp(scores - row_max), 0.0)
        total = lax.optimization_barrier(jnp.sum(probs, -1, keepdims=True))
        weights = probs.astype(jnp.bfloat16)
        return jnp.dot(weights, values, preferred_element_type=jnp.float32) / total
    outputs = lax.map(one_head, (query.transpose(1, 0, 2), keyval.transpose(1, 0, 2)))
    attended = outputs.transpose(1, 0, 2).reshape(count, HEADS * VDIM).astype(jnp.bfloat16)
    return jnp.dot(attended, w_out, preferred_element_type=jnp.float32).astype(jnp.bfloat16)
```

```python
import math

import jax
import jax.numpy as jnp
from jax import lax
from jax.sharding import PartitionSpec as P

NOPE = 128
ROPE = 64
VDIM = 128
KVRANK = 512


def rotate(pairs, position):
    half = pairs.shape[-1] // 2
    freqs = jnp.exp(
        jnp.arange(half, dtype=jnp.float32) * (-2.0 * math.log(10000.0) / pairs.shape[-1])
    )
    angle = position[..., None] * freqs
    first_half = pairs[..., :half]
    second_half = pairs[..., half:]
    return jnp.concatenate(
        [
            first_half * jnp.cos(angle) - second_half * jnp.sin(angle),
            first_half * jnp.sin(angle) + second_half * jnp.cos(angle),
        ],
        -1,
    )


def finish(compressed, position, latent_gain):
    lat_part = compressed[:, :KVRANK]
    latent = (
        lat_part * lax.rsqrt(jnp.mean(lat_part * lat_part, -1, keepdims=True) + 1e-06) * latent_gain
    ).astype(jnp.bfloat16)
    rope_key = rotate(compressed[:, KVRANK:], position).astype(jnp.bfloat16)
    return (latent, rope_key)


def body(hidden, q_latent, w_down, latent_gain, w_qup, w_kvup, w_out):
    tok_count = q_latent.shape[0]
    first = lax.axis_index("ctx") * tok_count
    position = (first + jnp.arange(tok_count, dtype=jnp.int32)).astype(jnp.float32)
    q_all = lax.all_gather(q_latent, "ctx", axis=0, tiled=True)
    partial_sum = jnp.dot(hidden, w_down, preferred_element_type=jnp.float32)
    compressed = lax.psum(partial_sum, "head")
    latent, rope_key = finish(compressed, position, latent_gain)
    both = lax.all_gather(jnp.concatenate([latent, rope_key], -1), "ctx", axis=0, tiled=True)
    latent, rope_key = both[:, :KVRANK], both[:, KVRANK:]
    width = NOPE + ROPE
    total_tok = both.shape[0]
    heads_here = w_qup.shape[1] // width
    all_index = jnp.arange(total_tok, dtype=jnp.int32)
    query = jnp.dot(q_all, w_qup, preferred_element_type=jnp.float32).reshape(
        total_tok, heads_here, width
    )
    query = jnp.concatenate(
        [query[..., :NOPE], rotate(query[..., NOPE:], all_index.astype(jnp.float32)[:, None])], -1
    ).astype(jnp.bfloat16)
    scale = width ** (-0.5)
    grouped = (
        jnp.dot(latent, w_kvup, preferred_element_type=jnp.float32)
        .astype(jnp.bfloat16)
        .reshape(total_tok, heads_here, NOPE + VDIM)
    )
    keys = jnp.concatenate(
        [
            grouped[..., :NOPE],
            jnp.broadcast_to(rope_key[:, None], (total_tok, heads_here, ROPE)),
        ],
        -1,
    )
    step = min(total_tok, 512)
    pieces = []
    for start in range(0, total_tok, step):
        stop = start + step
        scores = jnp.einsum(
            "thd,nhd->htn", query[start:stop], keys[:stop], preferred_element_type=jnp.float32
        )
        allowed = (all_index[None, :stop] <= all_index[start:stop, None])[None]
        scores = jnp.where(allowed, scores * scale, -1e30)
        probs = jnp.where(allowed, jnp.exp(scores - jnp.max(scores, -1, keepdims=True)), 0.0)
        total = jnp.sum(probs, -1)
        accum = jnp.einsum(
            "htn,nhv->thv",
            probs.astype(jnp.bfloat16),
            grouped[:stop, :, NOPE:],
            preferred_element_type=jnp.float32,
        )
        pieces.append((accum / total.T[..., None]).astype(jnp.bfloat16))
    attended = jnp.concatenate(pieces, 0).reshape(total_tok, heads_here * VDIM)
    terms = jnp.dot(attended, w_out, preferred_element_type=jnp.float32)
    return lax.psum_scatter(terms.astype(jnp.bfloat16), "head", scatter_dimension=0, tiled=True)


def solution(mesh):
    in_specs = (
        P(("groups", "ctx"), "head"),
        P(("groups", "ctx"), None),
        P("head", None),
        P(),
        P(None, "head"),
        P(None, "head"),
        P("head", "ctx"),
    )
    out_specs = P(("groups", "head"), "ctx")
    return jax.shard_map(body, mesh=mesh, in_specs=in_specs, out_specs=out_specs, check_vma=False)
```

```python
import functools
import math

import jax
import jax.numpy as jnp
import numpy as np
from jax import lax
from jax.experimental import pallas as pl
from jax.experimental.pallas import tpu as pltpu
from jax.sharding import PartitionSpec as P

NOPE = 128
ROPE = 64
VDIM = 128
KVRANK = 512
MESH = pl.DeviceIdType.MESH
F32 = jnp.float32
BF16 = jnp.bfloat16


def tables(count):
    half = ROPE // 2
    freqs = np.exp(np.arange(half, dtype=np.float32) * np.float32(-2.0 * math.log(10000.0) / ROPE))
    angle = np.arange(count, dtype=np.float32)[:, None] * freqs.astype(np.float32)[None]
    cos = np.cos(angle.astype(np.float64)).astype(np.float32)
    sin = np.sin(angle.astype(np.float64)).astype(np.float32)
    one, zero = np.ones((count, 64), np.float32), np.zeros((count, 64), np.float32)
    return (
        np.concatenate([cos, cos, one, one, cos, cos], 1),
        np.concatenate([-sin, sin, zero, zero, -sin, sin], 1),
    )


def kernel(
    C, H, hid, ql, wd, gain, wq, wkv, wo, cos_h, sin_h, out,
    hid_v, wd_v, wq_v, wkv_v, wo_v, cos_v, sin_v, qlat, part, rs, lat, q_s, kk, vv, att,
    terms, precv, xs, xr, load_sem, q_sem, lat_sem, rs_sem, p_sem, x_sem, send_sem,
):
    X = H // 2
    c, h = lax.axis_index("ctx"), lax.axis_index("head")
    core = lax.rem(h, 2)
    chip = lax.div(h, 2)
    mate = h + 1 - 2 * core
    tok = ql.shape[0]
    sub = tok // H
    T = C * tok
    pairs = q_s.shape[0]
    sends = []

    def load(i, src, dst):
        copy = pltpu.make_async_copy(src, dst, load_sem.at[i])
        copy.start()
        return copy

    own_q = load(0, ql, qlat.at[pl.ds(0, tok)])
    load_hid = load(1, hid, hid_v)
    load_wd = load(2, wd, wd_v)
    load_cos = load(3, cos_h, cos_v)
    load_sin = load(4, sin_h, sin_v)
    load_wq = load(5, wq, wq_v)
    load_wkv = load(6, wkv, wkv_v)
    load_wo = load(7, wo, wo_v)

    barrier = pltpu.get_barrier_semaphore()
    for d in range(1, C):
        pl.semaphore_signal(
            barrier, inc=1, device_id={"ctx": lax.rem(c + d, C)}, device_id_type=MESH
        )
    for e in range(1, H):
        pl.semaphore_signal(
            barrier, inc=1, device_id={"head": lax.rem(h + e, H)}, device_id_type=MESH
        )

    def remote(src, dst, sem, device):
        copy = pltpu.make_async_remote_copy(
            src_ref=src,
            dst_ref=dst,
            send_sem=send_sem.at[len(sends)],
            recv_sem=sem,
            device_id=device,
            device_id_type=MESH,
        )
        copy.start()
        sends.append(copy)

    def arrived(dst, sem):
        pltpu.make_async_copy(dst, dst, sem).wait()

    def rows(slot, hh):
        return pl.ds(pl.multiple_of(slot * tok + hh * sub, sub), sub)

    own_q.wait()
    pl.semaphore_wait(barrier, C - 1 + H - 1)
    for d in range(1, C):
        remote(
            qlat.at[rows(0, h)],
            qlat.at[rows(C - d, h)],
            q_sem.at[(C - d) * H + h],
            {"ctx": lax.rem(c + d, C)},
        )

    load_hid.wait()
    load_wd.wait()
    part[...] = jnp.dot(hid_v[...], wd_v[...], preferred_element_type=F32).reshape(part.shape)
    for e in range(1, H):
        to = lax.rem(h + e, H)
        remote(part.at[to], rs.at[e], rs_sem.at[e], {"head": to})

    lane = lax.broadcasted_iota(jnp.int32, (1, 128), 1)
    first = lax.rem(lane, 64) < 32
    low = lane < 64

    def project(slot, count):
        def group(jj, _):
            f = jnp.dot(
                qlat[slot * tok : (slot + count) * tok, :],
                wq_v[:, pl.ds(pl.multiple_of(jj * 768, 768), 768)],
                preferred_element_type=F32,
            )
            for s in range(count):
                true = pl.ds(pl.multiple_of(lax.rem(c + slot + s, C) * tok, tok), tok)
                for p in range(2):
                    piece = f[s * tok : (s + 1) * tok, p * 384 : (p + 1) * 384]
                    q_s[2 * jj + p, true, 0:128] = piece[:, :128].astype(BF16)
                    for w in range(2):
                        v = piece[:, 128 * (w + 1) : 128 * (w + 2)]
                        swapped = jnp.where(first, pltpu.roll(v, 96, 1), pltpu.roll(v, 32, 1))
                        side = slice(128 * w, 128 * (w + 1))
                        v = v * cos_v[true, side] + swapped * sin_v[true, side]
                        q_s[2 * jj + p, true, 128 * (w + 1) : 128 * (w + 2)] = v.astype(BF16)
            return 0

        lax.fori_loop(0, pairs // 2, group, 0)

    load_cos.wait()
    load_sin.wait()
    load_wq.wait()
    project(0, 1)

    for e in range(1, H):
        arrived(rs.at[e], rs_sem.at[e])
    total = part[h]
    for e in range(1, H):
        total = total + rs[e]
    lp = total[:, :KVRANK]
    latent = lp * lax.rsqrt(jnp.mean(lp * lp, -1, keepdims=True) + 1e-06) * gain[...]
    here = pl.ds(pl.multiple_of(c * tok + h * sub, sub), sub)
    a = total[:, KVRANK : KVRANK + 32]
    b = total[:, KVRANK + 32 : KVRANK + 64]
    cs, sn = cos_v[here, 0:32], sin_v[here, 32:64]
    ra, rb = a * cs - b * sn, a * sn + b * cs
    lat[here, 0:KVRANK] = latent.astype(BF16)
    lat[here, KVRANK:] = jnp.concatenate([ra, rb, ra, rb], -1).astype(BF16)

    def share_lat(cc, hh, device):
        r = rows(cc, hh)
        remote(lat.at[r], lat.at[r], lat_sem.at[cc * H + hh], device)

    def share_q(slot, hh, device):
        r = rows(slot, hh)
        remote(qlat.at[r], qlat.at[r], q_sem.at[slot * H + hh], device)

    def across(e):
        return lax.rem(h + 2 * e, H)

    for d in range(1, C):
        share_lat(c, h, {"ctx": lax.rem(c + d, C)})
    for e in range(1, X):
        share_lat(c, h, {"head": across(e)})
    share_lat(c, h, {"head": mate})

    for s in list(range(1, C)):
        arrived(qlat.at[rows(s, h)], q_sem.at[s * H + h])
        for e in range(1, X):
            share_q(s, h, {"head": across(e)})
        share_q(s, h, {"head": mate})
    for d in range(1, C):
        cc = lax.rem(c + d, C)
        arrived(lat.at[rows(cc, h)], lat_sem.at[cc * H + h])
        for e in range(1, X):
            share_lat(cc, h, {"head": across(e)})
        share_lat(cc, h, {"head": mate})
    for s in range(1, C):
        for e in range(1, X):
            hh = across(e)
            arrived(qlat.at[rows(s, hh)], q_sem.at[s * H + hh])
            share_q(s, hh, {"head": mate})
    for d in range(C):
        cc = lax.rem(c + d, C)
        for e in range(1, X):
            hh = across(e)
            arrived(lat.at[rows(cc, hh)], lat_sem.at[cc * H + hh])
            share_lat(cc, hh, {"head": mate})
    for s in range(1, C):
        for e in range(X):
            hh = lax.rem(mate + 2 * e, H)
            arrived(qlat.at[rows(s, hh)], q_sem.at[s * H + hh])
    step = max(n for n in (1, 2, 3) if (C - 1) % n == 0)
    for s in range(1, C, step):
        project(s, step)
    for d in range(C):
        cc = lax.rem(c + d, C)
        for e in range(X):
            hh = lax.rem(mate + 2 * e, H)
            arrived(lat.at[rows(cc, hh)], lat_sem.at[cc * H + hh])

    load_wkv.wait()
    span = min(T, 512)

    def keyval(j, _):
        for r0 in range(0, T, span):
            r = slice(r0, r0 + span)
            f = jnp.dot(
                lat[r, 0:KVRANK],
                wkv_v[:, pl.ds(pl.multiple_of(j * 512, 512), 512)],
                preferred_element_type=F32,
            )
            rk = lat[r, KVRANK:].astype(F32)
            kk[2 * j, r, 0:128] = f[:, 0:128].astype(BF16)
            kk[2 * j, r, 128:256] = jnp.where(low, rk, 0.0).astype(BF16)
            vv[2 * j, r, :] = f[:, 128:256].astype(BF16)
            k1 = pltpu.roll(f[:, 256:384], 64, 1)
            kk[2 * j + 1, r, 0:128] = jnp.where(low, 0.0, k1).astype(BF16)
            kk[2 * j + 1, r, 128:256] = jnp.where(low, k1, rk).astype(BF16)
            vv[2 * j + 1, r, :] = f[:, 384:512].astype(BF16)
        return 0

    lax.fori_loop(0, pairs, keyval, 0)

    R = T // X
    small = min(R, 256)
    factor = (NOPE + ROPE) ** (-0.5) * math.log2(math.e)

    def attend(bb):
        for r0 in range(0, R, small):
            start = bb * R + r0
            nk = start + small
            allowed = lax.broadcasted_iota(jnp.int32, (small, nk), 1) <= (
                lax.broadcasted_iota(jnp.int32, (small, nk), 0) + start
            )

            def pair(j, _):
                for i in range(2):
                    s = lax.dot_general(
                        q_s[j, start:nk, 128 * i : 128 * i + 256],
                        kk[2 * j + i, 0:nk, :],
                        (((1,), (1,)), ((), ())),
                        preferred_element_type=F32,
                    )
                    s = jnp.where(allowed, s, -1e30)
                    p = jnp.exp2((s - jnp.max(s, -1, keepdims=True)) * factor)
                    o = jnp.dot(p.astype(BF16), vv[2 * j + i, 0:nk, :], preferred_element_type=F32)
                    o = o / jnp.sum(p, -1, keepdims=True)
                    at = pl.ds(pl.multiple_of(j * 256 + i * 128, 128), 128)
                    att[r0 : r0 + small, at] = o.astype(BF16)
                return 0

            lax.fori_loop(0, pairs, pair, 0)

    chunks, _, sub2, nc = precv.shape[1:2] + (0,) + precv.shape[2:]

    def finish(t, n):
        arrived(precv.at[t, n], p_sem.at[t * chunks + n])
        value = terms[t, n, core].astype(F32) + precv[t, n].astype(F32)
        if t < X - 1:
            xs[t, n] = value.astype(BF16)
            remote(
                xs.at[t, n],
                xr.at[t, n],
                x_sem.at[t * chunks + n],
                {"head": lax.rem(h + 2 * (1 + t), H)},
            )
            return
        for u in range(X - 1):
            arrived(xr.at[u, n], x_sem.at[u * chunks + n])
            value = value + xr[u, n].astype(F32)
        out[:, n * nc : (n + 1) * nc] = value.astype(BF16)

    for t in range(X):
        block = lax.rem(chip + 1 + t, X)
        for bb in range(X):
            pl.when(block == bb)(functools.partial(attend, bb))
        if t == 0:
            load_wo.wait()
        for n in range(chunks):
            f = jnp.dot(att[...], wo_v[:, n * nc : (n + 1) * nc], preferred_element_type=F32)
            terms[t, n] = f.astype(BF16).reshape(2, sub2, nc)
            remote(
                terms.at[t, n, 1 - core], precv.at[t, n], p_sem.at[t * chunks + n], {"head": mate}
            )
            if n:
                finish(t, n - 1)
        finish(t, chunks - 1)
    for copy in sends:
        copy.wait_send()


def body(C, H, hidden, q_latent, w_down, latent_gain, w_qup, w_kvup, w_out):
    tok, rank = q_latent.shape
    T, X = C * tok, H // 2
    heads = w_qup.shape[1] // (NOPE + ROPE)
    cols = w_out.shape[1]
    nc = 256 if cols % 256 == 0 else cols
    chunks = cols // nc
    sub, sub2 = tok // H, T // H
    cos, sin = tables(T)
    wide = KVRANK + ROPE
    n_send = (C - 1) * (2 + X - 1 + X) + C * (X - 1 + X) + H - 1 + X * chunks + (X - 1) * chunks
    dma = pltpu.SemaphoreType.DMA
    hbm = pl.BlockSpec(memory_space=pl.ANY)
    vmem = pl.BlockSpec(memory_space=pltpu.VMEM)
    return pl.pallas_call(
        functools.partial(kernel, C, H),
        out_shape=jax.ShapeDtypeStruct((sub2, cols), BF16),
        in_specs=[hbm, hbm, hbm, vmem, hbm, hbm, hbm, hbm, hbm],
        out_specs=vmem,
        scratch_shapes=[
            pltpu.VMEM(hidden.shape, BF16),
            pltpu.VMEM(w_down.shape, BF16),
            pltpu.VMEM(w_qup.shape, BF16),
            pltpu.VMEM(w_kvup.shape, BF16),
            pltpu.VMEM(w_out.shape, BF16),
            pltpu.VMEM((T, 256), F32),
            pltpu.VMEM((T, 256), F32),
            pltpu.VMEM((T, rank), BF16),
            pltpu.VMEM((H, sub, wide), F32),
            pltpu.VMEM((H, sub, wide), F32),
            pltpu.VMEM((T, KVRANK + 128), BF16),
            pltpu.VMEM((heads // 2, T, 384), BF16),
            pltpu.VMEM((heads, T, 256), BF16),
            pltpu.VMEM((heads, T, VDIM), BF16),
            pltpu.VMEM((T // X, heads * VDIM), BF16),
            pltpu.VMEM((X, chunks, 2, sub2, nc), BF16),
            pltpu.VMEM((X, chunks, sub2, nc), BF16),
            pltpu.VMEM((X - 1, chunks, sub2, nc), BF16),
            pltpu.VMEM((X - 1, chunks, sub2, nc), BF16),
            dma((8,)),
            dma((C * H,)),
            dma((C * H,)),
            dma((H,)),
            dma((X * chunks,)),
            dma((X * chunks,)),
            dma((n_send,)),
        ],
        compiler_params=pltpu.CompilerParams(
            collective_id=0, has_side_effects=True, vmem_limit_bytes=60 * 1024 * 1024
        ),
    )(
        hidden, q_latent, w_down, latent_gain.reshape(1, -1), w_qup, w_kvup, w_out,
        jnp.asarray(cos), jnp.asarray(sin),
    )


def solution(mesh):
    in_specs = (
        P(("groups", "ctx"), "head"),
        P(("groups", "ctx"), None),
        P("head", None),
        P(),
        P(None, "head"),
        P(None, "head"),
        P("head", "ctx"),
    )
    out_specs = P(("groups", "head"), "ctx")
    return jax.shard_map(
        functools.partial(body, mesh.shape["ctx"], mesh.shape["head"]),
        mesh=mesh,
        in_specs=in_specs,
        out_specs=out_specs,
        check_vma=False,
    )
```

```python
import functools
import math

import jax
import jax.numpy as jnp
import numpy as np
from jax import lax
from jax.experimental import pallas as pl
from jax.experimental.pallas import tpu as pltpu
from jax.sharding import PartitionSpec as P

NOPE = 128
ROPE = 64
VDIM = 128
KVRANK = 512
MESH = pl.DeviceIdType.MESH
F32 = jnp.float32
BF16 = jnp.bfloat16


def tables(count):
    half = ROPE // 2
    freqs = np.exp(np.arange(half, dtype=np.float32) * np.float32(-2.0 * math.log(10000.0) / ROPE))
    angle = np.arange(count, dtype=np.float32)[:, None] * freqs.astype(np.float32)[None]
    cos = np.cos(angle.astype(np.float64)).astype(np.float32)
    sin = np.sin(angle.astype(np.float64)).astype(np.float32)
    one, zero = np.ones((count, 64), np.float32), np.zeros((count, 64), np.float32)
    return (
        np.concatenate([cos, cos, one, one, cos, cos], 1),
        np.concatenate([-sin, sin, zero, zero, -sin, sin], 1),
    )


def kernel(
    C, H, hid, ql, wd, gain, wq, wkv, wo, cos_h, sin_h, out,
    hid_v, wd_v, wq_v, wkv_v, wo_v, cos_v, sin_v, qlat, part, rs, lat, q_s, kk, vv, att,
    terms, precv, xs, xr, load_sem, q_sem, lat_sem, rs_sem, p_sem, x_sem, send_sem,
):
    X = H // 2
    c, h = lax.axis_index("ctx"), lax.axis_index("head")
    core = lax.rem(h, 2)
    chip = lax.div(h, 2)
    mate = h + 1 - 2 * core
    tok = ql.shape[0]
    sub = tok // H
    T = C * tok
    pairs = q_s.shape[0]
    sends = []

    def load(i, src, dst):
        copy = pltpu.make_async_copy(src, dst, load_sem.at[i])
        copy.start()
        return copy

    own_q = load(0, ql, qlat.at[pl.ds(0, tok)])
    load_hid = load(1, hid, hid_v)
    load_wd = load(2, wd, wd_v)
    barrier = pltpu.get_barrier_semaphore()
    for d in range(1, C):
        pl.semaphore_signal(
            barrier, inc=1, device_id={"ctx": lax.rem(c + d, C)}, device_id_type=MESH
        )
    for e in range(1, H):
        pl.semaphore_signal(
            barrier, inc=1, device_id={"head": lax.rem(h + e, H)}, device_id_type=MESH
        )

    def remote(src, dst, sem, device):
        copy = pltpu.make_async_remote_copy(
            src_ref=src,
            dst_ref=dst,
            send_sem=send_sem.at[len(sends)],
            recv_sem=sem,
            device_id=device,
            device_id_type=MESH,
        )
        copy.start()
        sends.append(copy)

    def arrived(dst, sem):
        pltpu.make_async_copy(dst, dst, sem).wait()

    def rows(slot, hh):
        return pl.ds(pl.multiple_of(slot * tok + hh * sub, sub), sub)

    own_q.wait()
    pl.semaphore_wait(barrier, C - 1 + H - 1)
    for d in range(1, C):
        remote(
            qlat.at[rows(0, h)],
            qlat.at[rows(C - d, h)],
            q_sem.at[(C - d) * H + h],
            {"ctx": lax.rem(c + d, C)},
        )

    load_hid.wait()
    load_wd.wait()
    load_cos = load(3, cos_h, cos_v)
    load_sin = load(4, sin_h, sin_v)
    load_wq = load(5, wq, wq_v)
    load_wkv = load(6, wkv, wkv_v)
    load_wo = load(7, wo, wo_v)
    part[...] = lax.dot_general(
        hid_v[...], wd_v[...], (((1,), (1,)), ((), ())), preferred_element_type=F32
    ).reshape(part.shape)
    for e in range(1, H):
        to = lax.rem(h + e, H)
        remote(part.at[to], rs.at[e], rs_sem.at[e], {"head": to})

    lane = lax.broadcasted_iota(jnp.int32, (1, 128), 1)
    first = lax.rem(lane, 64) < 32
    low = lane < 64

    def project(slot, count):
        def group(jj, _):
            f = jnp.dot(
                qlat[slot * tok : (slot + count) * tok, :],
                wq_v[:, pl.ds(pl.multiple_of(jj * 768, 768), 768)],
                preferred_element_type=F32,
            )
            for s in range(count):
                true = pl.ds(pl.multiple_of(lax.rem(c + slot + s, C) * tok, tok), tok)
                for p in range(2):
                    piece = f[s * tok : (s + 1) * tok, p * 384 : (p + 1) * 384]
                    q_s[2 * jj + p, true, 0:128] = piece[:, :128].astype(BF16)
                    for w in range(2):
                        v = piece[:, 128 * (w + 1) : 128 * (w + 2)]
                        swapped = jnp.where(first, pltpu.roll(v, 96, 1), pltpu.roll(v, 32, 1))
                        side = slice(128 * w, 128 * (w + 1))
                        v = v * cos_v[true, side] + swapped * sin_v[true, side]
                        q_s[2 * jj + p, true, 128 * (w + 1) : 128 * (w + 2)] = v.astype(BF16)
            return 0

        lax.fori_loop(0, pairs // 2, group, 0)

    load_cos.wait()
    load_sin.wait()
    load_wq.wait()
    project(0, 1)

    for e in range(1, H):
        arrived(rs.at[e], rs_sem.at[e])
    total = part[h]
    for e in range(1, H):
        total = total + rs[e]
    lp = total[:, :KVRANK]
    latent = lp * lax.rsqrt(jnp.mean(lp * lp, -1, keepdims=True) + 1e-06) * gain[...]
    here = pl.ds(pl.multiple_of(c * tok + h * sub, sub), sub)
    a = total[:, KVRANK : KVRANK + 32]
    b = total[:, KVRANK + 32 : KVRANK + 64]
    cs, sn = cos_v[here, 0:32], sin_v[here, 32:64]
    ra, rb = a * cs - b * sn, a * sn + b * cs
    lat[here, 0:KVRANK] = latent.astype(BF16)
    lat[here, KVRANK:] = jnp.concatenate([ra, rb, ra, rb], -1).astype(BF16)

    def share_lat(cc, hh, device):
        r = rows(cc, hh)
        remote(lat.at[r], lat.at[r], lat_sem.at[cc * H + hh], device)

    def share_q(slot, hh, device):
        r = rows(slot, hh)
        remote(qlat.at[r], qlat.at[r], q_sem.at[slot * H + hh], device)

    def across(e):
        return lax.rem(h + 2 * e, H)

    for d in range(1, C):
        share_lat(c, h, {"ctx": lax.rem(c + d, C)})
    for e in range(1, X):
        share_lat(c, h, {"head": across(e)})
    share_lat(c, h, {"head": mate})

    for s in range(1, C):
        arrived(qlat.at[rows(s, h)], q_sem.at[s * H + h])
        for e in range(1, X):
            share_q(s, h, {"head": across(e)})
        share_q(s, h, {"head": mate})
    for d in range(1, C):
        cc = lax.rem(c + d, C)
        arrived(lat.at[rows(cc, h)], lat_sem.at[cc * H + h])
        for e in range(1, X):
            share_lat(cc, h, {"head": across(e)})
        share_lat(cc, h, {"head": mate})
    for s in range(1, C):
        for e in range(1, X):
            hh = across(e)
            arrived(qlat.at[rows(s, hh)], q_sem.at[s * H + hh])
            share_q(s, hh, {"head": mate})
    for d in range(C):
        cc = lax.rem(c + d, C)
        for e in range(1, X):
            hh = across(e)
            arrived(lat.at[rows(cc, hh)], lat_sem.at[cc * H + hh])
            share_lat(cc, hh, {"head": mate})
    for s in range(1, C):
        for e in range(X):
            hh = lax.rem(mate + 2 * e, H)
            arrived(qlat.at[rows(s, hh)], q_sem.at[s * H + hh])
    step = max(n for n in (1, 2, 3) if (C - 1) % n == 0)
    for s in range(1, C, step):
        project(s, step)
    for d in range(C):
        cc = lax.rem(c + d, C)
        for e in range(X):
            hh = lax.rem(mate + 2 * e, H)
            arrived(lat.at[rows(cc, hh)], lat_sem.at[cc * H + hh])

    load_wkv.wait()
    span = min(T, 512)

    def keyval(j, _):
        for r0 in range(0, T, span):
            r = slice(r0, r0 + span)
            f = jnp.dot(
                lat[r, 0:KVRANK],
                wkv_v[:, pl.ds(pl.multiple_of(j * 512, 512), 512)],
                preferred_element_type=F32,
            )
            rk = lat[r, KVRANK:].astype(F32)
            kk[2 * j, r, 0:128] = f[:, 0:128].astype(BF16)
            kk[2 * j, r, 128:256] = jnp.where(low, rk, 0.0).astype(BF16)
            vv[2 * j, r, :] = f[:, 128:256].astype(BF16)
            k1 = pltpu.roll(f[:, 256:384], 64, 1)
            kk[2 * j + 1, r, 0:128] = jnp.where(low, 0.0, k1).astype(BF16)
            kk[2 * j + 1, r, 128:256] = jnp.where(low, k1, rk).astype(BF16)
            vv[2 * j + 1, r, :] = f[:, 384:512].astype(BF16)
        return 0

    lax.fori_loop(0, pairs, keyval, 0)

    R = T // X
    small = min(R, 256)
    factor = (NOPE + ROPE) ** (-0.5) * math.log2(math.e)

    def attend(bb):
        for r0 in range(0, R, small):
            start = bb * R + r0
            nk = start + small
            allowed = lax.broadcasted_iota(jnp.int32, (small, small), 1) <= (
                lax.broadcasted_iota(jnp.int32, (small, small), 0)
            )
            cuts = [(0, start), (start, nk)] if start else [(0, nk)]

            def pair(j, _):
                for i in range(2):
                    q = q_s[j, start:nk, 128 * i : 128 * i + 256]
                    s = [
                        lax.dot_general(
                            q,
                            kk[2 * j + i, lo:hi, :],
                            (((1,), (1,)), ((), ())),
                            preferred_element_type=F32,
                        )
                        for lo, hi in cuts
                    ]
                    s[-1] = jnp.where(allowed, s[-1], -1e30)
                    most = functools.reduce(jnp.maximum, [jnp.max(v, -1, keepdims=True) for v in s])
                    p = [jnp.exp2((v - most) * factor) for v in s]
                    total = sum(jnp.sum(v, -1, keepdims=True) for v in p)
                    o = sum(
                        jnp.dot(
                            v.astype(BF16), vv[2 * j + i, lo:hi, :], preferred_element_type=F32
                        )
                        for v, (lo, hi) in zip(p, cuts)
                    )
                    at = pl.ds(pl.multiple_of(j * 256 + i * 128, 128), 128)
                    att[r0 : r0 + small, at] = (o / total).astype(BF16)
                return 0

            lax.fori_loop(0, pairs, pair, 0, unroll=2 if T <= 512 else 1)

    chunks, _, sub2, nc = precv.shape[1:2] + (0,) + precv.shape[2:]

    def finish(t, n):
        arrived(precv.at[t, n], p_sem.at[t * chunks + n])
        value = terms[t, n, core].astype(F32) + precv[t, n].astype(F32)
        if t < X - 1:
            xs[t, n] = value.astype(BF16)
            remote(
                xs.at[t, n],
                xr.at[t, n],
                x_sem.at[t * chunks + n],
                {"head": lax.rem(h + 2 * (1 + t), H)},
            )
            return
        for u in range(X - 1):
            arrived(xr.at[u, n], x_sem.at[u * chunks + n])
            value = value + xr[u, n].astype(F32)
        out[:, n * nc : (n + 1) * nc] = value.astype(BF16)

    for t in range(X):
        block = lax.rem(chip + 1 + t, X)
        for bb in range(X):
            pl.when(block == bb)(functools.partial(attend, bb))
        if t == 0:
            load_wo.wait()
        for n in range(chunks):
            f = jnp.dot(att[...], wo_v[:, n * nc : (n + 1) * nc], preferred_element_type=F32)
            terms[t, n] = f.astype(BF16).reshape(2, sub2, nc)
            remote(
                terms.at[t, n, 1 - core], precv.at[t, n], p_sem.at[t * chunks + n], {"head": mate}
            )
            if n:
                finish(t, n - 1)
        finish(t, chunks - 1)
    for copy in sends:
        copy.wait_send()


def body(C, H, hidden, q_latent, w_down, latent_gain, w_qup, w_kvup, w_out):
    tok, rank = q_latent.shape
    T, X = C * tok, H // 2
    heads = w_qup.shape[1] // (NOPE + ROPE)
    cols = w_out.shape[1]
    nc = 256 if cols % 256 == 0 else cols
    chunks = cols // nc
    sub, sub2 = tok // H, T // H
    cos, sin = tables(T)
    wide = KVRANK + ROPE
    n_send = (C - 1) * (2 + X - 1 + X) + C * (X - 1 + X) + H - 1 + X * chunks + (X - 1) * chunks
    dma = pltpu.SemaphoreType.DMA
    hbm = pl.BlockSpec(memory_space=pl.ANY)
    vmem = pl.BlockSpec(memory_space=pltpu.VMEM)
    return pl.pallas_call(
        functools.partial(kernel, C, H),
        out_shape=jax.ShapeDtypeStruct((sub2, cols), BF16),
        in_specs=[hbm, hbm, hbm, vmem, hbm, hbm, hbm, hbm, hbm],
        out_specs=vmem,
        scratch_shapes=[
            pltpu.VMEM(hidden.shape, BF16),
            pltpu.VMEM(w_down.shape[::-1], BF16),
            pltpu.VMEM(w_qup.shape, BF16),
            pltpu.VMEM(w_kvup.shape, BF16),
            pltpu.VMEM(w_out.shape, BF16),
            pltpu.VMEM((T, 256), F32),
            pltpu.VMEM((T, 256), F32),
            pltpu.VMEM((T, rank), BF16),
            pltpu.VMEM((H, sub, wide), F32),
            pltpu.VMEM((H, sub, wide), F32),
            pltpu.VMEM((T, KVRANK + 128), BF16),
            pltpu.VMEM((heads // 2, T, 384), BF16),
            pltpu.VMEM((heads, T, 256), BF16),
            pltpu.VMEM((heads, T, VDIM), BF16),
            pltpu.VMEM((T // X, heads * VDIM), BF16),
            pltpu.VMEM((X, chunks, 2, sub2, nc), BF16),
            pltpu.VMEM((X, chunks, sub2, nc), BF16),
            pltpu.VMEM((X - 1, chunks, sub2, nc), BF16),
            pltpu.VMEM((X - 1, chunks, sub2, nc), BF16),
            dma((8,)),
            dma((C * H,)),
            dma((C * H,)),
            dma((H,)),
            dma((X * chunks,)),
            dma((X * chunks,)),
            dma((n_send,)),
        ],
        compiler_params=pltpu.CompilerParams(
            collective_id=0, has_side_effects=True, vmem_limit_bytes=60 * 1024 * 1024
        ),
    )(
        hidden, q_latent, w_down.T, latent_gain.reshape(1, -1), w_qup, w_kvup, w_out,
        jnp.asarray(cos), jnp.asarray(sin),
    )


def solution(mesh):
    in_specs = (
        P(("groups", "ctx"), "head"),
        P(("groups", "ctx"), None),
        P("head", None),
        P(),
        P(None, "head"),
        P(None, "head"),
        P("head", "ctx"),
    )
    out_specs = P(("groups", "head"), "ctx")
    return jax.shard_map(
        functools.partial(body, mesh.shape["ctx"], mesh.shape["head"]),
        mesh=mesh,
        in_specs=in_specs,
        out_specs=out_specs,
        check_vma=False,
    )
```
